128 devices in a mesh: rows: 64 (over x, y_lo, z, core), chan: 2 (over y_hi).
Axes of the slice: x: 4, y: 4 (y_hi: 2, y_lo: 2; y = y_hi * 2 + y_lo), z: 4, core: 2. Of those that a mesh axis runs over, the one named last changes fastest.
Arguments:
- spectra: bfloat16 [1024, 512, 2048], P('rows', None, 'chan'), may hold values from -40 to 40
- factors: bfloat16 [2048, 128], P('chan'), may hold values from -0.125 to 0.125
Outputs:
- scaled_gradient: float32 [128, 2048], P('rows', 'chan')
- objective: float32 [1], replicated
The draws below stay inside these ranges and needn't reach their ends.
All inputs are finite; a program needn't handle non-finite values.
Results may differ from the reference program's by a relative error of at most 0.0029.
Values may be sent and summed in bfloat16 or wider, within the bound.
A program may use at most 128 MiB of HBM per device.

```python
import math
import jax
import jax.numpy as jnp
from jax import lax

C = 2048
K = 128
WP = 512
H = 1024


def draw_spectra(key, part):
    base_key = jax.random.fold_in(key, 11)
    noise_key, jitter_key, channel_key = jax.random.split(base_key, 3)
    row_pos = jnp.arange(H, dtype=jnp.float32)
    ramp = jnp.exp(math.log(3.0) * row_pos / float(max(H - 1, 1)))
    jitter = jnp.exp(jax.random.uniform(jitter_key, (H,), jnp.float32, math.log(0.5), math.log(1.6)))
    channel_scale = jnp.exp(jax.random.uniform(channel_key, (C,), jnp.float32, math.log(0.2), math.log(2.0)))
    values = jax.random.truncated_normal(noise_key, -4.0, 4.0, (H, WP, C), jnp.float32)
    scaled = values * (ramp * jitter)[:, None, None] * channel_scale[None, None, :]
    return scaled.astype(jnp.bfloat16)


def block_levels(rng, shape, cuts, smallest, top_value):
    loudness, own = 1.0, jax.random.fold_in(rng, 6)
    for position, parts in cuts:
        draws = jnp.exp(jax.random.uniform(jax.random.fold_in(own, position), (parts,), jnp.float32, smallest / len(cuts), top_value / len(cuts)))
        loudness = loudness * jnp.repeat(draws, shape[position] // parts).reshape([-1 if axis == position else 1 for axis in range(len(shape))])
    return loudness


def normal_values(stream_key, dims, spread, most, shards=(), kind=jnp.bfloat16):
    loudness = block_levels(stream_key, dims, shards, -0.22, 0.18) if shards else 1.0
    drawn = jax.random.normal(stream_key, dims, jnp.float32) * spread * loudness
    return jnp.minimum(jnp.maximum(drawn, -most), most).astype(kind)


def setup_inputs(seed: int = 0) -> dict:
    key_of = jax.random.split(jax.random.key(seed), 3)
    spectra = draw_spectra(jax.random.fold_in(key_of[2], 71), 0)
    factors = normal_values(key_of[1], (C, K), C ** -0.5, 0.125, ((0, 2),))
    return {"spectra": spectra, "factors": factors}


def reference(spectra, factors):
    loadings = factors.astype(jnp.float32)

    def row_scores(row_data):
        return jnp.dot(row_data.astype(jnp.float32), loadings)

    scores = lax.map(row_scores, spectra)
    npix = float(H * WP)
    column_mean = jnp.sum(scores, axis=(0, 1)) / npix
    centered = scores - column_mean
    cov_total = jnp.sum(centered * centered) / npix
    padded = jnp.pad(scores, ((4, 4), (0, 0), (0, 0)))
    row_index = jnp.arange(H, dtype=jnp.int32)
    variogram = jnp.float32(0.0)
    lag_grad = jnp.zeros_like(scores)
    for distance in range(1, 5):
        ahead_rows = padded[4 + distance:4 + distance + H]
        behind_rows = padded[4 - distance:4 - distance + H]
        fwd_ok = (row_index + distance < H).astype(jnp.float32)[:, None, None]
        back_ok = (row_index >= distance).astype(jnp.float32)[:, None, None]
        forward_diff = (ahead_rows - scores) * fwd_ok
        pair_count = float((H - distance) * WP)
        variogram = variogram + jnp.sum(forward_diff * forward_diff) / (2.0 * pair_count)
        lag_grad = lag_grad + ((scores - behind_rows) * back_ok - forward_diff) / pair_count
    weights = (npix * lag_grad / cov_total - 2.0 * variogram * centered / (cov_total * cov_total)).astype(jnp.bfloat16)

    def accumulate(total, pair):
        weight_row, data_row = pair
        return total + jnp.dot(weight_row.astype(jnp.float32).T, data_row.astype(jnp.float32)), None

    start_total = jnp.zeros((K, C), jnp.float32)
    gradient_total, _ = lax.scan(accumulate, start_total, (weights, spectra))
    return gradient_total, (variogram / cov_total).reshape(1)
```

```python
import jax
import jax.numpy as jnp
from jax import lax
from jax.experimental import pallas as pl
from jax.experimental.pallas import tpu as pltpu
from jax.sharding import PartitionSpec as P

MESH = pl.DeviceIdType.MESH
F32, BF16 = jnp.float32, jnp.bfloat16

ROWS = 16
STRIPS = 64
WP = 512
HALF = 256
K = 128
CH = 1024
H = ROWS * STRIPS
NPIX = float(H * WP)
LAGS = (1, 2, 3, 4)
PAIRS = tuple(float((H - lag) * WP) for lag in LAGS)
SUB = 64


def device_of(x, y, z, core):
    return ((x * 2 + y % 2) * 4 + z) * 2 + core, y // 2


def fold(block):
    return jnp.sum(block.reshape(block.shape[0] // 8, 8, K), axis=0)


def kernel(
    x_hbm, f_hbm, g_out, obj_out,
    xv, fv, fp, s, psend, precv, hsend, hrecv, w, wrecv, mu, acc, tile, mom_a, mom_b, grad,
    red_z, red_x, part, red_b,
    x_sem, f_sem, p_ssem, p_rsem, h_ssem, h_rsem, ma_ssem, ma_rsem, mb_ssem, mb_rsem,
    w_ssem, w_rsem, z_ssem, z_rsem, xx_ssem, xx_rsem, b_ssem, b_rsem,
):
    strip = lax.axis_index("rows")
    chan = lax.axis_index("chan")
    core, z, ylo, xx = strip % 2, (strip // 2) % 4, (strip // 8) % 2, strip // 16
    y = chan * 2 + ylo
    mine = pl.multiple_of(chan * HALF, HALF)
    theirs = pl.multiple_of((1 - chan) * HALF, HALF)
    partner = (strip, 1 - chan)
    after = ((strip + 1) % STRIPS, chan)
    before = ((strip + STRIPS - 1) % STRIPS, chan)

    def order(i):
        return (i + 12) % ROWS

    def x_copy(i, own):
        r, at = order(i), mine if own else theirs
        return pltpu.make_async_copy(
            x_hbm.at[r, pl.ds(at, HALF), :],
            xv.at[r, pl.ds(at, HALF), :],
            x_sem.at[i + (ROWS if own else 0)],
        )

    f_copy = pltpu.make_async_copy(f_hbm, fv, f_sem)
    f_copy.start()

    @pl.loop(0, ROWS)
    def _(i):
        x_copy(i, False).start()
        x_copy(i, True).start()

    barrier = pltpu.get_barrier_semaphore()

    def greet(place):
        pl.semaphore_signal(barrier, inc=1, device_id=place, device_id_type=MESH)

    q = z * 2 + core
    t = xx * 4 + y
    u = xx * 2 + core

    def zc_peer(j):
        other = (q + j) % 8
        return device_of(xx, y, other // 2, other % 2)

    def xy_peer(j):
        other = (t + j) % 16
        return device_of(other // 4, other % 4, z, core)

    def xc_peer(j):
        other = (u + j) % 8
        return device_of(other // 2, y, z, other % 2)

    @pl.loop(1, 8)
    def _(j):
        greet(zc_peer(j))

    @pl.loop(1, 16)
    def _(j):
        greet(xy_peer(j))

    @pl.loop(1, 4)
    def _(j):
        greet(device_of((xx + j) % 4, y, z, 1 - core))
        greet(device_of(xx, chan * 2 + 1 - ylo, (z + j) % 4, core))

    greet(after)
    greet(before)

    f_copy.wait()
    src = lax.broadcasted_iota(jnp.int32, (K, K), 0)
    dst = lax.broadcasted_iota(jnp.int32, (K, K), 1)
    hi, mid, lo, e = dst >> 6, (dst >> 3) & 7, (dst >> 1) & 3, dst & 1
    to_x = jnp.where(hi == 0, lo, mid >> 1)
    to_z = jnp.where(hi == 0, mid >> 1, lo)
    from_k = (((to_x * 2 + hi) * 4 + to_z) * 2 + (mid & 1)) * 2 + e
    permutation = jnp.where(src == from_k, 1.0, 0.0).astype(BF16)
    fp[...] = jnp.dot(fv[...], permutation, preferred_element_type=F32).astype(BF16)

    def p_copy(r):
        return pltpu.make_async_remote_copy(
            psend.at[r], precv.at[r], p_ssem.at[r], p_rsem.at[r],
            device_id=partner, device_id_type=MESH,
        )

    @pl.loop(0, ROWS)
    def _(i):
        r = order(i)
        x_copy(i, False).wait()
        psend[r] = jnp.dot(
            xv[r, pl.ds(theirs, HALF), :], fp[...], preferred_element_type=F32
        ).astype(BF16)

        @pl.when(i == 0)
        def _():
            pl.semaphore_wait(barrier, 30)

        p_copy(r).start()
        x_copy(i, True).wait()
        s[4 + r] = jnp.dot(xv[r, pl.ds(mine, HALF), :], fp[...], preferred_element_type=F32)

    acc[...] = jnp.zeros_like(acc)

    def add_row(r, first=False):
        p_copy(r).wait_recv()
        if first:
            total = jnp.zeros((8, K), F32)
            for h in range(0, HALF, SUB):
                total += fold(s[4 + r, h : h + SUB, :] + precv[r, h : h + SUB, :].astype(F32))
            mu[...] = jnp.broadcast_to(
                jnp.sum(total, axis=0, keepdims=True) * (1.0 / HALF), (8, K)
            )
        shift = mu[0:1, :]
        one, two = jnp.zeros((8, K), F32), jnp.zeros((8, K), F32)
        for h in range(0, HALF, SUB):
            v = s[4 + r, h : h + SUB, :] + precv[r, h : h + SUB, :].astype(F32)
            s[4 + r, h : h + SUB, :] = v
            d = v - shift
            one += fold(d)
            two += fold(d * d)
        acc[0] += one
        acc[1] += two

    def add_lags(a, across=None):
        sums = [jnp.zeros((8, K), F32) for _ in LAGS]
        for h in range(0, HALF, SUB):
            here = s[4 + a, h : h + SUB, :]
            for n, lag in enumerate(LAGS):
                d = s[4 + a + lag, h : h + SUB, :] - here
                sums[n] += fold(d * d)
        for n, lag in enumerate(LAGS):
            inside = across is None or a + lag < ROWS
            acc[2 + n] += sums[n] if inside else sums[n] * across

    def h_copy(up):
        at, to, where = (4, 0, after) if up else (0, 4, before)
        n = 0 if up else 1
        return pltpu.make_async_remote_copy(
            hsend.at[pl.ds(at, 4)], hrecv.at[pl.ds(to, 4)], h_ssem.at[n], h_rsem.at[n],
            device_id=where, device_id_type=MESH,
        )

    add_row(12, first=True)

    @pl.loop(13, 16)
    def _(r):
        add_row(r)

    hsend[4:8] = s[16:20].astype(BF16)
    h_copy(True).start()

    @pl.loop(0, 4)
    def _(r):
        add_row(r)

    hsend[0:4] = s[4:8].astype(BF16)
    h_copy(False).start()

    @pl.loop(4, 11)
    def _(r):
        add_row(r)
        add_lags(r - 4)

    h_copy(False).wait_recv()
    s[20:24] = hrecv[4:8].astype(F32)
    inner = jnp.where(strip == STRIPS - 1, 0.0, 1.0).astype(F32)
    for a in range(12, 16):
        add_lags(a, inner)
    add_row(11)

    @pl.loop(7, 12)
    def _(a):
        add_lags(a)

    count = float(ROWS * HALF)
    drift = jnp.sum(acc[0], axis=0, keepdims=True) * (1.0 / count)
    tile[0:1] = mu[0:1, :] + drift
    tile[1:2] = jnp.sum(acc[1], axis=0, keepdims=True) - count * drift * drift
    for n in range(4):
        tile[2 + n : 3 + n] = jnp.sum(acc[2 + n], axis=0, keepdims=True)
    tile[6:8] = jnp.zeros((2, K), F32)

    def gather(size, me, peer, slots, send, recv):
        slots[me] = tile[...]

        def copy(j):
            return pltpu.make_async_remote_copy(
                tile, slots.at[me], send.at[j], recv.at[me],
                device_id=peer(j), device_id_type=MESH,
            )

        def arrival(j):
            slot = (me + j) % size
            return pltpu.make_async_remote_copy(
                tile, slots.at[slot], send.at[j], recv.at[slot],
                device_id=peer(j), device_id_type=MESH,
            )

        @pl.loop(1, size)
        def _(j):
            copy(j).start()

        @pl.loop(1, size)
        def _(j):
            arrival(j).wait_recv()

        @pl.loop(1, size)
        def _(j):
            copy(j).wait_send()

    def merge(slots, size, each):
        parts = [slots[n] for n in range(size)]
        total = parts[0]
        for part_ in parts[1:]:
            total = total + part_
        mean = total[0:1] * (1.0 / size)
        spread = jnp.zeros((1, K), F32)
        for part_ in parts:
            gap = part_[0:1] - mean
            spread += gap * gap
        return mean, total[1:2] + each * spread, total[2:6]

    gather(8, q, zc_peer, mom_a, ma_ssem, ma_rsem)
    mean, squares, lags = merge(mom_a, 8, count)
    tile[0:1] = mean
    tile[1:2] = squares
    tile[2:6] = lags
    gather(16, t, xy_peer, mom_b, mb_ssem, mb_rsem)
    mean, squares, lags = merge(mom_b, 16, 8 * count)
    cov = jnp.sum(squares, axis=1, keepdims=True) * (1.0 / NPIX)
    variogram = jnp.zeros((1, 1), F32)
    for n in range(4):
        variogram += jnp.sum(lags[n : n + 1], axis=1, keepdims=True) / (2.0 * PAIRS[n])
    objective = variogram / cov
    obj_out[0] = objective[0, 0]
    alpha = [jnp.broadcast_to((NPIX / n) / cov, (1, K)) for n in PAIRS]
    beta = jnp.broadcast_to(2.0 * objective / cov, (1, K))

    h_copy(True).wait_recv()
    s[0:4] = hrecv[0:4].astype(F32)

    def w_copy(r):
        return pltpu.make_async_remote_copy(
            w.at[r], wrecv.at[r], w_ssem.at[r], w_rsem.at[r],
            device_id=partner, device_id_type=MESH,
        )

    @pl.loop(0, ROWS)
    def _(r):
        row = strip * ROWS + r
        back = [alpha[n] * jnp.where(row >= lag, 1.0, 0.0) for n, lag in enumerate(LAGS)]
        ahead = [alpha[n] * jnp.where(row + lag < H, 1.0, 0.0) for n, lag in enumerate(LAGS)]
        for h in range(0, HALF, SUB):
            here = s[4 + r, h : h + SUB, :]
            value = beta * (mean - here)
            for n, lag in enumerate(LAGS):
                value += back[n] * (here - s[4 + r - lag, h : h + SUB, :])
                value += ahead[n] * (here - s[4 + r + lag, h : h + SUB, :])
            w[r, h : h + SUB, :] = value.astype(BF16)
        w_copy(r).start()

    grad[...] = jnp.zeros_like(grad)

    def add_grad(weights, data):
        grad[...] += lax.dot_general(
            weights, data, (((0,), (0,)), ((), ())), preferred_element_type=F32
        )

    @pl.loop(0, ROWS)
    def _(r):
        add_grad(w[r], xv[r, pl.ds(mine, HALF), :])

    @pl.loop(0, ROWS)
    def _(r):
        w_copy(r).wait_recv()
        add_grad(wrecv[r], xv[r, pl.ds(theirs, HALF), :])

    def z_copy(j, slot):
        return pltpu.make_async_remote_copy(
            grad.at[pl.ds(pl.multiple_of((q + j) % 8 * 8, 8), 8)], red_z.at[slot],
            z_ssem.at[j], z_rsem.at[slot], device_id=zc_peer(j), device_id_type=MESH,
        )

    def xx_copy(j, slot):
        return pltpu.make_async_remote_copy(
            grad.at[pl.ds(pl.multiple_of(64 + (u + j) % 8 * 8, 8), 8)], red_x.at[slot],
            xx_ssem.at[j], xx_rsem.at[slot], device_id=xc_peer(j), device_id_type=MESH,
        )

    @pl.loop(1, 8)
    def _(j):
        z_copy(j, q).start()
        xx_copy(j, u).start()

    red_z[q] = grad[pl.ds(pl.multiple_of(q * 8, 8), 8), :]
    red_x[u] = grad[pl.ds(pl.multiple_of(64 + u * 8, 8), 8), :]

    @pl.loop(1, 8)
    def _(j):
        z_copy(j, (q + j) % 8).wait_recv()
        xx_copy(j, (u + j) % 8).wait_recv()

    total_z, total_x = red_z[0], red_x[0]
    for n in range(1, 8):
        total_z = total_z + red_z[n]
        total_x = total_x + red_x[n]
    for n in range(4):
        part[n] = total_z[2 * n : 2 * n + 2, :]
        part[4 + n] = total_x[2 * n : 2 * n + 2, :]

    def bz_copy(j):
        to = (xx + j) % 4
        return pltpu.make_async_remote_copy(
            part.at[to], red_b.at[xx * 2 + ylo], b_ssem.at[j], b_rsem.at[xx * 2 + ylo],
            device_id=device_of(to, chan * 2, z, core), device_id_type=MESH,
        )

    def bx_copy(j):
        to = (z + j) % 4
        return pltpu.make_async_remote_copy(
            part.at[4 + to], red_b.at[z * 2 + ylo], b_ssem.at[4 + j], b_rsem.at[z * 2 + ylo],
            device_id=device_of(xx, chan * 2 + 1, to, core), device_id_type=MESH,
        )

    @pl.when(ylo == 0)
    def _():
        bx_copy(0).start()
        red_b[xx * 2] = part[xx]

    @pl.when(ylo == 1)
    def _():
        bz_copy(0).start()
        red_b[z * 2 + 1] = part[4 + z]

    for j in range(1, 4):
        bz_copy(j).start()
        bx_copy(j).start()
    own = jnp.where(ylo == 0, xx * 2, z * 2 + 1)

    @pl.loop(1, 8)
    def _(j):
        slot = (own + j) % 8
        pltpu.make_async_remote_copy(
            part.at[0], red_b.at[slot], b_ssem.at[0], b_rsem.at[slot],
            device_id=partner, device_id_type=MESH,
        ).wait_recv()

    total = red_b[0]
    for n in range(1, 8):
        total = total + red_b[n]
    g_out[...] = total

    @pl.loop(0, ROWS)
    def _(r):
        p_copy(r).wait_send()
        w_copy(r).wait_send()

    h_copy(True).wait_send()
    h_copy(False).wait_send()

    @pl.loop(1, 8)
    def _(j):
        z_copy(j, q).wait_send()
        xx_copy(j, u).wait_send()

    @pl.when(ylo == 0)
    def _():
        bx_copy(0).wait_send()

    @pl.when(ylo == 1)
    def _():
        bz_copy(0).wait_send()

    for j in range(1, 4):
        bz_copy(j).wait_send()
        bx_copy(j).wait_send()


def on_device(spectra, factors):
    dma = pltpu.SemaphoreType.DMA
    return pl.pallas_call(
        kernel,
        name="autocorrelation_gradient",
        out_shape=(
            jax.ShapeDtypeStruct((2, CH), F32),
            jax.ShapeDtypeStruct((1,), F32),
        ),
        in_specs=[pl.BlockSpec(memory_space=pl.ANY)] * 2,
        out_specs=(
            pl.BlockSpec(memory_space=pltpu.VMEM),
            pl.BlockSpec(memory_space=pltpu.SMEM),
        ),
        scratch_shapes=[
            pltpu.VMEM((ROWS, WP, CH), BF16),
            pltpu.VMEM((CH, K), BF16),
            pltpu.VMEM((CH, K), BF16),
            pltpu.VMEM((ROWS + 8, HALF, K), F32),
            pltpu.VMEM((ROWS, HALF, K), BF16),
            pltpu.VMEM((ROWS, HALF, K), BF16),
            pltpu.VMEM((8, HALF, K), BF16),
            pltpu.VMEM((8, HALF, K), BF16),
            pltpu.VMEM((ROWS, HALF, K), BF16),
            pltpu.VMEM((ROWS, HALF, K), BF16),
            pltpu.VMEM((8, K), F32),
            pltpu.VMEM((6, 8, K), F32),
            pltpu.VMEM((8, K), F32),
            pltpu.VMEM((8, 8, K), F32),
            pltpu.VMEM((16, 8, K), F32),
            pltpu.VMEM((K, CH), F32),
            pltpu.VMEM((8, 8, CH), F32),
            pltpu.VMEM((8, 8, CH), F32),
            pltpu.VMEM((8, 2, CH), F32),
            pltpu.VMEM((8, 2, CH), F32),
            dma((2 * ROWS,)),
            dma,
            dma((ROWS,)), dma((ROWS,)),
            dma((2,)), dma((2,)),
            dma((8,)), dma((8,)),
            dma((16,)), dma((16,)),
            dma((ROWS,)), dma((ROWS,)),
            dma((8,)), dma((8,)),
            dma((8,)), dma((8,)),
            dma((8,)), dma((8,)),
        ],
        compiler_params=pltpu.CompilerParams(
            collective_id=0, has_side_effects=True, vmem_limit_bytes=56 << 20
        ),
    )(spectra, factors)


def solution(mesh):
    return jax.shard_map(
        on_device,
        mesh=mesh,
        in_specs=(P("rows", None, "chan"), P("chan", None)),
        out_specs=(P("rows", "chan"), P()),
        check_vma=False,
    )
```

```python
import jax
import jax.numpy as jnp
from jax import lax
from jax.experimental import pallas as pl
from jax.experimental.pallas import tpu as pltpu
from jax.sharding import PartitionSpec as P

MESH = pl.DeviceIdType.MESH
F32, BF16 = jnp.float32, jnp.bfloat16

ROWS = 16
STRIPS = 64
WP = 512
HALF = 256
EXT = 128
REST = HALF - EXT
K = 128
CH = 1024
H = ROWS * STRIPS
NPIX = float(H * WP)
LAGS = (1, 2, 3, 4)
PAIRS = tuple(float((H - lag) * WP) for lag in LAGS)
AHEAD = 4
FLYING = 8
GOING = 4
SUB = 32


def device_of(x, y, z, core):
    return ((x * 2 + y % 2) * 4 + z) * 2 + core, y // 2


def fold(block):
    return jnp.sum(block.reshape(block.shape[0] // 8, 8, K), axis=0)


def kernel(
    x_hbm, f_hbm, g_out, obj_out,
    xo, xe, xt, fv, fp, s, se, psend, precv, pxsend, pxrecv, hsend, hrecv, hxsend, hxrecv,
    w, we, wrecv, mu, acc, tile, tile_b, mom_a, mom_b, grad,
    red_z, red_x, part, red_b,
    x_sem, f_sem, p_ssem, p_rsem, px_ssem, px_rsem, h_ssem, h_rsem, hx_ssem, hx_rsem, ma_ssem, ma_rsem, mb_ssem, mb_rsem,
    w_ssem, w_rsem, z_ssem, z_rsem, xx_ssem, xx_rsem, b_ssem, b_rsem,
):
    strip = lax.axis_index("rows")
    chan = lax.axis_index("chan")
    core, z, ylo, xx = strip % 2, (strip // 2) % 4, (strip // 8) % 2, strip // 16
    y = chan * 2 + ylo
    mine = pl.multiple_of(chan * HALF, HALF)
    theirs = pl.multiple_of((1 - chan) * HALF, HALF)
    partner = (strip, 1 - chan)
    after = ((strip + 1) % STRIPS, chan)
    before = ((strip + STRIPS - 1) % STRIPS, chan)

    def order(i):
        return i // 4 * 12 % ROWS + i % 4

    def x_copy(r, n):
        at, size, to = ((theirs, EXT, xe), (theirs + EXT, REST, xt), (mine, HALF, xo))[n]
        return pltpu.make_async_copy(
            x_hbm.at[r, pl.ds(pl.multiple_of(at, SUB), size), :],
            to.at[pl.ds(pl.multiple_of(r * size, SUB), size), :],
            x_sem.at[n, r],
        )

    f_copy = pltpu.make_async_copy(f_hbm, fv, f_sem)
    f_copy.start()

    for i in range(AHEAD):
        x_copy(order(i), 0).start()
        x_copy(order(i), 1).start()

    barrier = pltpu.get_barrier_semaphore()

    def greet(place):
        pl.semaphore_signal(barrier, inc=1, device_id=place, device_id_type=MESH)

    q = z * 2 + core
    t = xx * 4 + y
    u = xx * 2 + core

    def zc_peer(j):
        other = (q + j) % 8
        return device_of(xx, y, other // 2, other % 2)

    def xy_peer(j):
        other = (t + j) % 16
        return device_of(other // 4, other % 4, z, core)

    def xc_peer(j):
        other = (u + j) % 8
        return device_of(other // 2, y, z, other % 2)

    @pl.loop(1, 8)
    def _(j):
        greet(zc_peer(j))

    @pl.loop(1, 16)
    def _(j):
        greet(xy_peer(j))

    @pl.loop(1, 4)
    def _(j):
        greet(device_of((xx + j) % 4, y, z, 1 - core))
        greet(device_of(xx, chan * 2 + 1 - ylo, (z + j) % 4, core))

    greet(after)
    greet(before)
    greet(device_of((xx + 1) % 4, y, 3 - z, 1 - core))
    greet(device_of((xx + 3) % 4, y, 3 - z, 1 - core))

    f_copy.wait()
    src = lax.broadcasted_iota(jnp.int32, (K, K), 0)
    dst = lax.broadcasted_iota(jnp.int32, (K, K), 1)
    hi, mid, lo, e = dst >> 6, (dst >> 3) & 7, (dst >> 1) & 3, dst & 1
    to_x = jnp.where(hi == 0, lo, mid >> 1)
    to_z = jnp.where(hi == 0, mid >> 1, lo)
    from_k = (((to_x * 2 + hi) * 4 + to_z) * 2 + (mid & 1)) * 2 + e
    permutation = jnp.where(src == from_k, 1.0, 0.0).astype(BF16)
    fp[...] = jnp.dot(fv[...], permutation, preferred_element_type=F32).astype(BF16)

    def p_copy(r):
        return pltpu.make_async_remote_copy(
            psend.at[r], precv.at[r], p_ssem.at[r], p_rsem.at[r],
            device_id=partner, device_id_type=MESH,
        )

    def scores(ref, r, size):
        data = ref[pl.ds(pl.multiple_of(r * size, SUB), size), :]
        return jnp.dot(data, fp[...], preferred_element_type=F32)

    @pl.loop(0, ROWS)
    def _(i):
        r = order(i)

        @pl.when(i + AHEAD < ROWS)
        def _():
            x_copy(order(i + AHEAD), 0).start()
            x_copy(order(i + AHEAD), 1).start()

        x_copy(r, 2).start()
        x_copy(r, 0).wait()
        psend[r, 0:EXT, :] = scores(xe, r, EXT).astype(BF16)
        x_copy(r, 1).wait()
        psend[r, EXT:HALF, :] = scores(xt, r, REST).astype(BF16)

        @pl.when(i == 0)
        def _():
            pl.semaphore_wait(barrier, 32)

        @pl.when(i < FLYING)
        def _():
            p_copy(r).start()

    acc[...] = jnp.zeros_like(acc)

    def add_row(i, first=False):
        r = order(i)
        p_copy(r).wait_send()

        @pl.when(i + FLYING < ROWS)
        def _():
            p_copy(order(i + FLYING)).start()

        x_copy(r, 2).wait()
        s[4 + r] = scores(xo, r, HALF)
        pxsend[r] = s[4 + r, 0:EXT, :].astype(BF16)
        p_copy(r).wait_recv()
        if first:
            total = jnp.zeros((8, K), F32)
            for h in range(0, HALF, SUB):
                total += fold(s[4 + r, h : h + SUB, :] + precv[r, h : h + SUB, :].astype(F32))
            mu[...] = jnp.broadcast_to(
                jnp.sum(total, axis=0, keepdims=True) * (1.0 / HALF), (8, K)
            )
        shift = mu[0:1, :]
        one, two = jnp.zeros((8, K), F32), jnp.zeros((8, K), F32)
        for h in range(0, HALF, SUB):
            v = s[4 + r, h : h + SUB, :] + precv[r, h : h + SUB, :].astype(F32)
            s[4 + r, h : h + SUB, :] = v
            d = v - shift
            one += fold(d)
            two += fold(d * d)
        acc[0] += one
        acc[1] += two

    def add_lags(a, across=None):
        sums = [jnp.zeros((8, K), F32) for _ in LAGS]
        for h in range(0, HALF, SUB):
            here = s[4 + a, h : h + SUB, :]
            for n, lag in enumerate(LAGS):
                d = s[4 + a + lag, h : h + SUB, :] - here
                sums[n] += fold(d * d)
        for n, lag in enumerate(LAGS):
            inside = across is None or a + lag < ROWS
            acc[2 + n] += sums[n] if inside else sums[n] * across

    class Halo:
        def __init__(self, size, send, hold, send_sem, recv_sem):
            self.size, self.send, self.hold, self.sems = size, send, hold, (send_sem, recv_sem)

        def copy(self, up, n, hop, source, slot, place):
            way = 0 if up else 1
            return pltpu.make_async_remote_copy(
                source, self.held(up, n, slot),
                self.sems[0].at[way, hop, n], self.sems[1].at[way, slot, n],
                device_id=place, device_id_type=MESH,
            )

        def held(self, up, n, slot):
            return self.hold.at[slot, pl.ds((0 if up else 4) + n * self.size, self.size)]

        def first(self, up, n, far=False):
            source = self.send.at[pl.ds((4 if up else 0) + n * self.size, self.size)]
            if far and (not up or self.size == 4):
                return self.copy(up, n, 0, source, 0, after if up else before)
            if far:
                return self.copy(up, n, 0, source, 1, device_of(xx, chan * 2 + 1 - ylo, z, core))
            return self.copy(up, n, 0, source, 0, zc_peer(1 if up else 7))

        def second(self, n):
            place = device_of((xx + 1 - ylo) % 4, y, 0, 0)
            return self.copy(True, n, 1, self.held(True, n, 1), 0, place)

        def end(self, up):
            return (z == 3) & (core == 1) if up else (z == 0) & (core == 0)

        def start(self, up, n=0):
            @pl.when(self.end(up))
            def _():
                self.first(up, n, far=True).start()

            @pl.when(jnp.logical_not(self.end(up)))
            def _():
                self.first(up, n).start()

        def arrive(self, up, n=0, slot=0):
            self.copy(up, n, 0, self.held(up, n, slot), slot, partner).wait_recv()

        def relay(self, n=0):
            @pl.when(self.end(True))
            def _():
                self.arrive(True, n, 1)
                self.second(n).start()

        def drain(self, up):
            @pl.loop(0, 4 // self.size)
            def _(n):
                self.first(up, n).wait_send()
                if not up or self.size == 4:
                    return

                @pl.when(self.end(up))
                def _():
                    self.second(n).wait_send()

    halo = Halo(1, hsend, hrecv, h_ssem, h_rsem)
    halo_ext = Halo(4, hxsend, hxrecv, hx_ssem, hx_rsem)
    UP, DOWN = True, False

    def px_copy(n):
        return pltpu.make_async_remote_copy(
            pxsend.at[pl.ds(n * 4, 4)], pxrecv.at[pl.ds(n * 4, 4)], px_ssem.at[n], px_rsem.at[n],
            device_id=partner, device_id_type=MESH,
        )

    def send_down(n):
        hsend[n] = s[4 + n].astype(BF16)
        halo.start(DOWN, n)

    add_row(0, first=True)
    send_down(0)

    @pl.loop(1, 4)
    def _(n):
        add_row(n)
        send_down(n)

    @pl.loop(0, 4)
    def _(n):
        add_row(4 + n)
        hsend[4 + n] = s[16 + n].astype(BF16)
        halo.start(UP, n)

    @pl.loop(0, 4)
    def _(n):
        add_row(8 + n)

    @pl.loop(8, 12)
    def _(a):
        add_lags(a)

    @pl.loop(0, 3)
    def _(n):
        add_row(12 + n)
        add_lags(n)

    px_copy(0).start()
    for n in range(4):
        halo.arrive(DOWN, n)
    s[20:24] = hrecv[0, 4:8].astype(F32)
    inner = jnp.where(strip == STRIPS - 1, 0.0, 1.0).astype(F32)
    for a in range(12, 16):
        add_lags(a, inner)
    add_row(15)
    px_copy(3).start()

    @pl.loop(3, 8)
    def _(a):
        add_lags(a)

    count = float(ROWS * HALF)
    drift = jnp.sum(acc[0], axis=0, keepdims=True) * (1.0 / count)
    tile[0:1] = mu[0:1, :] + drift
    tile[1:2] = jnp.sum(acc[1], axis=0, keepdims=True) - count * drift * drift
    for n in range(4):
        tile[2 + n : 3 + n] = jnp.sum(acc[2 + n], axis=0, keepdims=True)
    tile[6:8] = jnp.zeros((2, K), F32)

    def gather(tile, size, me, peer, slots, send, recv, beside):
        slots[me] = tile[...]

        def copies(source, target, place):
            return pltpu.make_async_remote_copy(
                source, target, send, recv, device_id=place, device_id_type=MESH
            )

        @pl.loop(1, size)
        def _(j):
            copies(tile, slots.at[me], peer(j)).start()

        px_copy(beside).start()
        others = slots.at[pl.ds(0, size - 1)]
        copies(others, others, partner).wait_recv()
        return copies(others, others, partner)

    def merge(slots, size, each):
        parts = [slots[n] for n in range(size)]
        total = parts[0]
        for part_ in parts[1:]:
            total = total + part_
        mean = total[0:1] * (1.0 / size)
        spread = jnp.zeros((1, K), F32)
        for part_ in parts:
            gap = part_[0:1] - mean
            spread += gap * gap
        return mean, total[1:2] + each * spread, total[2:6]

    sent_a = gather(tile, 8, q, zc_peer, mom_a, ma_ssem, ma_rsem, 2)
    mean, squares, lags = merge(mom_a, 8, count)
    tile_b[0:1] = mean
    tile_b[1:2] = squares
    tile_b[2:6] = lags
    tile_b[6:8] = jnp.zeros((2, K), F32)
    sent_b = gather(tile_b, 16, t, xy_peer, mom_b, mb_ssem, mb_rsem, 1)
    mean, squares, lags = merge(mom_b, 16, 8 * count)
    cov = jnp.sum(squares, axis=1, keepdims=True) * (1.0 / NPIX)
    variogram = jnp.zeros((1, 1), F32)
    for n in range(4):
        variogram += jnp.sum(lags[n : n + 1], axis=1, keepdims=True) / (2.0 * PAIRS[n])
    objective = variogram / cov
    obj_out[0] = objective[0, 0]
    alpha = [jnp.broadcast_to((NPIX / n) / cov, (1, K)) for n in PAIRS]
    beta = jnp.broadcast_to(2.0 * objective / cov, (1, K))

    for n in range(4):
        halo.relay(n)

    def w_copy(r):
        return pltpu.make_async_remote_copy(
            w.at[pl.ds(pl.multiple_of(r * HALF + EXT, SUB), REST)],
            wrecv.at[pl.ds(pl.multiple_of(r * REST, SUB), REST)], w_ssem.at[r], w_rsem.at[r],
            device_id=partner, device_id_type=MESH,
        )

    def weigh(r, source, target, size):
        row = strip * ROWS + r
        back = [alpha[n] * jnp.where(row >= lag, 1.0, 0.0) for n, lag in enumerate(LAGS)]
        ahead = [alpha[n] * jnp.where(row + lag < H, 1.0, 0.0) for n, lag in enumerate(LAGS)]
        for h in range(0, size, SUB):
            here = source[4 + r, h : h + SUB, :]
            value = beta * (mean - here)
            for n, lag in enumerate(LAGS):
                value += back[n] * (here - source[4 + r - lag, h : h + SUB, :])
                value += ahead[n] * (here - source[4 + r + lag, h : h + SUB, :])
            target[pl.ds(pl.multiple_of(r * size + h, SUB), SUB), :] = value.astype(BF16)

    def go(k):
        w_copy((k + 4) % ROWS).start()

    def tick(k):
        w_copy((k + 4) % ROWS).wait_send()
        go(k + GOING)

    @pl.loop(0, 8)
    def _(k):
        weigh(k + 4, s, w, HALF)

        @pl.when(k < GOING)
        def _():
            go(k)

    for n in range(4):
        halo.arrive(UP, n)
    s[0:4] = hrecv[0, 0:4].astype(F32)

    @pl.loop(0, 4)
    def _(n):
        weigh(12 + n, s, w, HALF)
        tick(n)

    pl.loop(0, 4)(lambda n: weigh(n, s, w, HALF))

    for n in range(4):
        px_copy(n).wait_recv()

    @pl.loop(0, ROWS)
    def _(r):
        se[4 + r] = psend[r, 0:EXT, :].astype(F32) + pxrecv[r].astype(F32)

    hxsend[0:4] = se[4:8].astype(BF16)
    hxsend[4:8] = se[16:20].astype(BF16)
    halo_ext.start(DOWN)
    halo_ext.start(UP)
    grad[...] = jnp.zeros_like(grad)

    def add_grad(weights, data):
        grad[...] += lax.dot_general(
            weights, data, (((0,), (0,)), ((), ())), preferred_element_type=F32
        )

    def own_grad(n):
        some = pl.ds(pl.multiple_of(n * CH, CH), CH)
        add_grad(w[some, :], xo[some, :])

    def rest_grad(start, rows):
        for r in range(start, start + rows):
            w_copy(r).wait_recv()
        some = slice(start * REST, (start + rows) * REST)
        add_grad(wrecv[some, :], xt[some, :])

    @pl.loop(0, 2)
    def _(n):
        own_grad(n)
        tick(4 + n)

    @pl.loop(2, 4)
    def _(n):
        own_grad(n)
        tick(4 + n)

    rest_grad(4, 4)
    tick(8)
    tick(9)
    tick(10)
    tick(11)
    rest_grad(8, 4)
    halo_ext.arrive(DOWN)
    halo_ext.arrive(UP)
    se[20:24] = hxrecv[0, 4:8].astype(F32)
    se[0:4] = hxrecv[0, 0:4].astype(F32)

    @pl.loop(0, ROWS)
    def _(r):
        weigh(r, se, we, EXT)

    add_grad(we[...], xe[...])
    for start, rows in ((12, 4), (0, 2), (2, 1), (3, 1)):
        rest_grad(start, rows)

    def z_copy(j):
        return pltpu.make_async_remote_copy(
            grad.at[pl.ds(pl.multiple_of((q + j) % 8 * 8, 8), 8)], red_z.at[q],
            z_ssem, z_rsem, device_id=zc_peer(j), device_id_type=MESH,
        )

    def xx_copy(j):
        return pltpu.make_async_remote_copy(
            grad.at[pl.ds(pl.multiple_of(64 + (u + j) % 8 * 8, 8), 8)], red_x.at[u],
            xx_ssem, xx_rsem, device_id=xc_peer(j), device_id_type=MESH,
        )

    def seven(ref, send, recv):
        some = ref.at[pl.ds(0, 7)]
        return pltpu.make_async_remote_copy(
            some, some, send, recv, device_id=partner, device_id_type=MESH
        )

    @pl.loop(1, 8)
    def _(j):
        z_copy(j).start()
        xx_copy(j).start()

    red_z[q] = grad[pl.ds(pl.multiple_of(q * 8, 8), 8), :]
    red_x[u] = grad[pl.ds(pl.multiple_of(64 + u * 8, 8), 8), :]

    seven(red_z, z_ssem, z_rsem).wait_recv()
    seven(red_x, xx_ssem, xx_rsem).wait_recv()
    total_z, total_x = red_z[0], red_x[0]
    for n in range(1, 8):
        total_z = total_z + red_z[n]
        total_x = total_x + red_x[n]
    for n in range(4):
        part[n] = total_z[2 * n : 2 * n + 2, :]
        part[4 + n] = total_x[2 * n : 2 * n + 2, :]

    def bz_copy(j):
        to = (xx + j) % 4
        return pltpu.make_async_remote_copy(
            part.at[to], red_b.at[xx * 2 + ylo], b_ssem, b_rsem,
            device_id=device_of(to, chan * 2, z, core), device_id_type=MESH,
        )

    def bx_copy(j):
        to = (z + j) % 4
        return pltpu.make_async_remote_copy(
            part.at[4 + to], red_b.at[z * 2 + ylo], b_ssem, b_rsem,
            device_id=device_of(xx, chan * 2 + 1, to, core), device_id_type=MESH,
        )

    @pl.when(ylo == 0)
    def _():
        bx_copy(0).start()
        red_b[xx * 2] = part[xx]

    @pl.when(ylo == 1)
    def _():
        bz_copy(0).start()
        red_b[z * 2 + 1] = part[4 + z]

    for j in range(1, 4):
        bz_copy(j).start()
        bx_copy(j).start()
    seven(red_b, b_ssem, b_rsem).wait_recv()
    total = red_b[0]
    for n in range(1, 8):
        total = total + red_b[n]
    g_out[...] = total

    sent_a.wait_send()
    sent_b.wait_send()

    @pl.loop(0, 4)
    def _(r):
        w_copy(r).wait_send()

    for n in range(4):
        px_copy(n).wait_send()
    for up in (False, True):
        halo.drain(up)
        halo_ext.drain(up)

    seven(red_z, z_ssem, z_rsem).wait_send()
    seven(red_x, xx_ssem, xx_rsem).wait_send()
    seven(red_b, b_ssem, b_rsem).wait_send()


def on_device(spectra, factors):
    dma = pltpu.SemaphoreType.DMA
    return pl.pallas_call(
        kernel,
        name="autocorrelation_gradient",
        out_shape=(
            jax.ShapeDtypeStruct((2, CH), F32),
            jax.ShapeDtypeStruct((1,), F32),
        ),
        in_specs=[pl.BlockSpec(memory_space=pl.ANY)] * 2,
        out_specs=(
            pl.BlockSpec(memory_space=pltpu.VMEM),
            pl.BlockSpec(memory_space=pltpu.SMEM),
        ),
        scratch_shapes=[
            pltpu.VMEM((ROWS * HALF, CH), BF16),
            pltpu.VMEM((ROWS * EXT, CH), BF16),
            pltpu.VMEM((ROWS * REST, CH), BF16),
            pltpu.VMEM((CH, K), BF16),
            pltpu.VMEM((CH, K), BF16),
            pltpu.VMEM((ROWS + 8, HALF, K), F32),
            pltpu.VMEM((ROWS + 8, EXT, K), F32),
            pltpu.VMEM((ROWS, HALF, K), BF16),
            pltpu.VMEM((ROWS, HALF, K), BF16),
            pltpu.VMEM((ROWS, EXT, K), BF16),
            pltpu.VMEM((ROWS, EXT, K), BF16),
            pltpu.VMEM((8, HALF, K), BF16),
            pltpu.VMEM((2, 8, HALF, K), BF16),
            pltpu.VMEM((8, EXT, K), BF16),
            pltpu.VMEM((2, 8, EXT, K), BF16),
            pltpu.VMEM((ROWS * HALF, K), BF16),
            pltpu.VMEM((ROWS * EXT, K), BF16),
            pltpu.VMEM((ROWS * REST, K), BF16),
            pltpu.VMEM((8, K), F32),
            pltpu.VMEM((6, 8, K), F32),
            pltpu.VMEM((8, K), F32),
            pltpu.VMEM((8, K), F32),
            pltpu.VMEM((8, 8, K), F32),
            pltpu.VMEM((16, 8, K), F32),
            pltpu.VMEM((K, CH), F32),
            pltpu.VMEM((8, 8, CH), F32),
            pltpu.VMEM((8, 8, CH), F32),
            pltpu.VMEM((8, 2, CH), F32),
            pltpu.VMEM((8, 2, CH), F32),
            dma((3, ROWS)),
            dma,
            dma((ROWS,)), dma((ROWS,)),
            dma((4,)), dma((4,)),
            dma((2, 2, 4)), dma((2, 2, 4)),
            dma((2, 2, 1)), dma((2, 2, 1)),
            dma, dma,
            dma, dma,
            dma((ROWS,)), dma((ROWS,)),
            dma, dma,
            dma, dma,
            dma, dma,
        ],
        compiler_params=pltpu.CompilerParams(
            collective_id=0, has_side_effects=True, vmem_limit_bytes=56 << 20
        ),
    )(spectra, factors)


def solution(mesh):
    return jax.shard_map(
        on_device,
        mesh=mesh,
        in_specs=(P("rows", None, "chan"), P("chan", None)),
        out_specs=(P("rows", "chan"), P()),
        check_vma=False,
    )
```

```python
import jax
import jax.numpy as jnp
from jax import lax
from jax.experimental import pallas as pl
from jax.experimental.pallas import tpu as pltpu
from jax.sharding import PartitionSpec as P

MESH = pl.DeviceIdType.MESH
F32, BF16 = jnp.float32, jnp.bfloat16

ROWS = 16
STRIPS = 64
WP = 512
HALF = 256
EXT = 128
REST = HALF - EXT
K = 128
CH = 1024
H = ROWS * STRIPS
NPIX = float(H * WP)
LAGS = (1, 2, 3, 4)
PAIRS = tuple(float((H - lag) * WP) for lag in LAGS)
AHEAD = 4
FLYING = 8
GOING = 6
SUB = 32


def device_of(x, y, z, core):
    return ((x * 2 + y % 2) * 4 + z) * 2 + core, y // 2


def fold(block):
    return jnp.sum(block.reshape(block.shape[0] // 8, 8, K), axis=0)


def kernel(
    x_hbm, f_hbm, g_out, obj_out,
    xo, xe, xt, fv, fp, s, se, psend, precv, pxsend, pxrecv, hsend, hrecv, hxsend, hxrecv,
    w, we, wrecv, mu, acc, tile, tile_b, mom_a, mom_b, grad,
    red_z, red_x, part, red_b, late, piece, late_z, late_x,
    x_sem, f_sem, p_ssem, p_rsem, px_ssem, px_rsem, h_ssem, h_rsem, hx_ssem, hx_rsem, ma_ssem, ma_rsem, mb_ssem, mb_rsem,
    w_ssem, w_rsem, z_ssem, z_rsem, xx_ssem, xx_rsem, b_ssem, b_rsem,
    lz_ssem, lz_rsem, lx_ssem, lx_rsem,
):
    strip = lax.axis_index("rows")
    chan = lax.axis_index("chan")
    core, z, ylo, xx = strip % 2, (strip // 2) % 4, (strip // 8) % 2, strip // 16
    y = chan * 2 + ylo
    mine = pl.multiple_of(chan * HALF, HALF)
    theirs = pl.multiple_of((1 - chan) * HALF, HALF)
    partner = (strip, 1 - chan)
    after = ((strip + 1) % STRIPS, chan)
    before = ((strip + STRIPS - 1) % STRIPS, chan)

    def order(i):
        return i // 4 * 12 % ROWS + i % 4

    def x_copy(r, n):
        at, size, to = ((theirs, EXT, xe), (theirs + EXT, REST, xt), (mine, HALF, xo))[n]
        return pltpu.make_async_copy(
            x_hbm.at[r, pl.ds(pl.multiple_of(at, SUB), size), :],
            to.at[pl.ds(pl.multiple_of(r * size, SUB), size), :],
            x_sem.at[n, r],
        )

    f_copy = pltpu.make_async_copy(f_hbm, fv, f_sem)
    f_copy.start()

    for i in range(AHEAD):
        x_copy(order(i), 0).start()
        x_copy(order(i), 1).start()

    barrier = pltpu.get_barrier_semaphore()

    def greet(place):
        pl.semaphore_signal(barrier, inc=1, device_id=place, device_id_type=MESH)

    q = z * 2 + core
    t = xx * 4 + y
    u = xx * 2 + core

    def zc_peer(j):
        other = (q + j) % 8
        return device_of(xx, y, other // 2, other % 2)

    def xy_peer(j):
        other = (t + j) % 16
        return device_of(other // 4, other % 4, z, core)

    def xc_peer(j):
        other = (u + j) % 8
        return device_of(other // 2, y, z, other % 2)

    @pl.loop(1, 8)
    def _(j):
        greet(zc_peer(j))

    @pl.loop(1, 16)
    def _(j):
        greet(xy_peer(j))

    @pl.loop(1, 4)
    def _(j):
        greet(device_of((xx + j) % 4, y, z, 1 - core))
        greet(device_of(xx, chan * 2 + 1 - ylo, (z + j) % 4, core))

    greet(after)
    greet(before)
    greet(device_of((xx + 1) % 4, y, 3 - z, 1 - core))
    greet(device_of((xx + 3) % 4, y, 3 - z, 1 - core))

    f_copy.wait()
    src = lax.broadcasted_iota(jnp.int32, (K, K), 0)
    dst = lax.broadcasted_iota(jnp.int32, (K, K), 1)
    hi, mid, lo, e = dst >> 6, (dst >> 3) & 7, (dst >> 1) & 3, dst & 1
    to_x = jnp.where(hi == 0, lo, mid >> 1)
    to_z = jnp.where(hi == 0, mid >> 1, lo)
    from_k = (((to_x * 2 + hi) * 4 + to_z) * 2 + (mid & 1)) * 2 + e
    permutation = jnp.where(src == from_k, 1.0, 0.0).astype(BF16)
    fp[...] = jnp.dot(fv[...], permutation, preferred_element_type=F32).astype(BF16)

    def p_copy(r):
        return pltpu.make_async_remote_copy(
            psend.at[r], precv.at[r], p_ssem.at[r], p_rsem.at[r],
            device_id=partner, device_id_type=MESH,
        )

    def scores(ref, r, size):
        data = ref[pl.ds(pl.multiple_of(r * size, SUB), size), :]
        return jnp.dot(data, fp[...], preferred_element_type=F32)

    @pl.loop(0, ROWS)
    def _(i):
        r = order(i)

        @pl.when(i + AHEAD < ROWS)
        def _():
            x_copy(order(i + AHEAD), 0).start()
            x_copy(order(i + AHEAD), 1).start()

        x_copy(r, 2).start()
        x_copy(r, 0).wait()
        psend[r, 0:EXT, :] = scores(xe, r, EXT).astype(BF16)
        x_copy(r, 1).wait()
        psend[r, EXT:HALF, :] = scores(xt, r, REST).astype(BF16)

        @pl.when(i == 0)
        def _():
            pl.semaphore_wait(barrier, 32)

        @pl.when(i < FLYING)
        def _():
            p_copy(r).start()

    acc[...] = jnp.zeros_like(acc)

    def add_row(i, first=False):
        r = order(i)
        p_copy(r).wait_send()

        @pl.when(i + FLYING < ROWS)
        def _():
            p_copy(order(i + FLYING)).start()

        x_copy(r, 2).wait()
        s[4 + r] = scores(xo, r, HALF)
        pxsend[r] = s[4 + r, 0:EXT, :].astype(BF16)
        p_copy(r).wait_recv()
        if first:
            total = jnp.zeros((8, K), F32)
            for h in range(0, HALF, SUB):
                total += fold(s[4 + r, h : h + SUB, :] + precv[r, h : h + SUB, :].astype(F32))
            mu[...] = jnp.broadcast_to(
                jnp.sum(total, axis=0, keepdims=True) * (1.0 / HALF), (8, K)
            )
        shift = mu[0:1, :]
        one, two = jnp.zeros((8, K), F32), jnp.zeros((8, K), F32)
        for h in range(0, HALF, SUB):
            v = s[4 + r, h : h + SUB, :] + precv[r, h : h + SUB, :].astype(F32)
            s[4 + r, h : h + SUB, :] = v
            d = v - shift
            one += fold(d)
            two += fold(d * d)
        acc[0] += one
        acc[1] += two

    def add_lags(a, across=None):
        sums = [jnp.zeros((8, K), F32) for _ in LAGS]
        for h in range(0, HALF, SUB):
            here = s[4 + a, h : h + SUB, :]
            for n, lag in enumerate(LAGS):
                d = s[4 + a + lag, h : h + SUB, :] - here
                sums[n] += fold(d * d)
        for n, lag in enumerate(LAGS):
            inside = across is None or a + lag < ROWS
            acc[2 + n] += sums[n] if inside else sums[n] * across

    class Halo:
        def __init__(self, size, send, hold, send_sem, recv_sem):
            self.size, self.send, self.hold, self.sems = size, send, hold, (send_sem, recv_sem)

        def copy(self, up, n, hop, source, slot, place):
            way = 0 if up else 1
            return pltpu.make_async_remote_copy(
                source, self.held(up, n, slot),
                self.sems[0].at[way, hop, n], self.sems[1].at[way, slot, n],
                device_id=place, device_id_type=MESH,
            )

        def held(self, up, n, slot):
            return self.hold.at[slot, pl.ds((0 if up else 4) + n * self.size, self.size)]

        def first(self, up, n, far=False):
            source = self.send.at[pl.ds((4 if up else 0) + n * self.size, self.size)]
            if far and (not up or self.size == 4):
                return self.copy(up, n, 0, source, 0, after if up else before)
            if far:
                return self.copy(up, n, 0, source, 1, device_of(xx, chan * 2 + 1 - ylo, z, core))
            return self.copy(up, n, 0, source, 0, zc_peer(1 if up else 7))

        def second(self, n):
            place = device_of((xx + 1 - ylo) % 4, y, 0, 0)
            return self.copy(True, n, 1, self.held(True, n, 1), 0, place)

        def end(self, up):
            return (z == 3) & (core == 1) if up else (z == 0) & (core == 0)

        def start(self, up, n=0):
            @pl.when(self.end(up))
            def _():
                self.first(up, n, far=True).start()

            @pl.when(jnp.logical_not(self.end(up)))
            def _():
                self.first(up, n).start()

        def arrive(self, up, n=0, slot=0):
            self.copy(up, n, 0, self.held(up, n, slot), slot, partner).wait_recv()

        def relay(self, n=0):
            @pl.when(self.end(True))
            def _():
                self.arrive(True, n, 1)
                self.second(n).start()

        def drain(self, up):
            @pl.loop(0, 4 // self.size)
            def _(n):
                self.first(up, n).wait_send()
                if not up or self.size == 4:
                    return

                @pl.when(self.end(up))
                def _():
                    self.second(n).wait_send()

    halo = Halo(1, hsend, hrecv, h_ssem, h_rsem)
    halo_ext = Halo(4, hxsend, hxrecv, hx_ssem, hx_rsem)
    UP, DOWN = True, False

    def px_copy(n):
        return pltpu.make_async_remote_copy(
            pxsend.at[pl.ds(n * 4, 4)], pxrecv.at[pl.ds(n * 4, 4)], px_ssem.at[n], px_rsem.at[n],
            device_id=partner, device_id_type=MESH,
        )

    def send_down(n):
        hsend[n] = s[4 + n].astype(BF16)
        halo.start(DOWN, n)

    add_row(0, first=True)
    send_down(0)

    @pl.loop(1, 4)
    def _(n):
        add_row(n)
        send_down(n)

    @pl.loop(0, 4)
    def _(n):
        add_row(4 + n)
        hsend[4 + n] = s[16 + n].astype(BF16)
        halo.start(UP, n)

    @pl.loop(0, 4)
    def _(n):
        add_row(8 + n)

    @pl.loop(8, 12)
    def _(a):
        add_lags(a)

    @pl.loop(0, 3)
    def _(n):
        add_row(12 + n)
        add_lags(n)

    px_copy(0).start()
    for n in range(4):
        halo.arrive(DOWN, n)
    s[20:24] = hrecv[0, 4:8].astype(F32)
    inner = jnp.where(strip == STRIPS - 1, 0.0, 1.0).astype(F32)
    for a in range(12, 16):
        add_lags(a, inner)
    add_row(15)
    px_copy(3).start()

    @pl.loop(3, 8)
    def _(a):
        add_lags(a)

    count = float(ROWS * HALF)
    drift = jnp.sum(acc[0], axis=0, keepdims=True) * (1.0 / count)
    tile[0:1] = mu[0:1, :] + drift
    tile[1:2] = jnp.sum(acc[1], axis=0, keepdims=True) - count * drift * drift
    for n in range(4):
        tile[2 + n : 3 + n] = jnp.sum(acc[2 + n], axis=0, keepdims=True)
    tile[6:8] = jnp.zeros((2, K), F32)

    def gather(tile, size, me, peer, slots, send, recv, beside):
        slots[me] = tile[...]

        def copies(source, target, place):
            return pltpu.make_async_remote_copy(
                source, target, send, recv, device_id=place, device_id_type=MESH
            )

        @pl.loop(1, size)
        def _(j):
            copies(tile, slots.at[me], peer(j)).start()

        px_copy(beside).start()
        others = slots.at[pl.ds(0, size - 1)]
        copies(others, others, partner).wait_recv()
        return copies(others, others, partner)

    def merge(slots, size, each):
        parts = [slots[n] for n in range(size)]
        total = parts[0]
        for part_ in parts[1:]:
            total = total + part_
        mean = total[0:1] * (1.0 / size)
        spread = jnp.zeros((1, K), F32)
        for part_ in parts:
            gap = part_[0:1] - mean
            spread += gap * gap
        return mean, total[1:2] + each * spread, total[2:6]

    sent_a = gather(tile, 8, q, zc_peer, mom_a, ma_ssem, ma_rsem, 2)
    mean, squares, lags = merge(mom_a, 8, count)
    tile_b[0:1] = mean
    tile_b[1:2] = squares
    tile_b[2:6] = lags
    tile_b[6:8] = jnp.zeros((2, K), F32)
    sent_b = gather(tile_b, 16, t, xy_peer, mom_b, mb_ssem, mb_rsem, 1)
    mean, squares, lags = merge(mom_b, 16, 8 * count)
    cov = jnp.sum(squares, axis=1, keepdims=True) * (1.0 / NPIX)
    variogram = jnp.zeros((1, 1), F32)
    for n in range(4):
        variogram += jnp.sum(lags[n : n + 1], axis=1, keepdims=True) / (2.0 * PAIRS[n])
    objective = variogram / cov
    obj_out[0] = objective[0, 0]
    alpha = [jnp.broadcast_to((NPIX / n) / cov, (1, K)) for n in PAIRS]
    beta = jnp.broadcast_to(2.0 * objective / cov, (1, K))

    for n in range(4):
        halo.relay(n)

    def w_copy(r):
        return pltpu.make_async_remote_copy(
            w.at[pl.ds(pl.multiple_of(r * HALF + EXT, SUB), REST)],
            wrecv.at[pl.ds(pl.multiple_of(r * REST, SUB), REST)], w_ssem.at[r], w_rsem.at[r],
            device_id=partner, device_id_type=MESH,
        )

    def weigh(r, source, target, size):
        row = strip * ROWS + r
        back = [alpha[n] * jnp.where(row >= lag, 1.0, 0.0) for n, lag in enumerate(LAGS)]
        ahead = [alpha[n] * jnp.where(row + lag < H, 1.0, 0.0) for n, lag in enumerate(LAGS)]
        for h in range(0, size, SUB):
            here = source[4 + r, h : h + SUB, :]
            value = beta * (mean - here)
            for n, lag in enumerate(LAGS):
                value += back[n] * (here - source[4 + r - lag, h : h + SUB, :])
                value += ahead[n] * (here - source[4 + r + lag, h : h + SUB, :])
            target[pl.ds(pl.multiple_of(r * size + h, SUB), SUB), :] = value.astype(BF16)

    def go(k):
        w_copy((k + 4) % ROWS).start()

    def tick(k):
        w_copy((k + 4) % ROWS).wait_send()
        if isinstance(k, int):
            if k + GOING < ROWS:
                go(k + GOING)
        else:
            pl.when(k + GOING < ROWS)(lambda: go(k + GOING))

    @pl.loop(0, 8)
    def _(k):
        weigh(k + 4, s, w, HALF)

        @pl.when(k < GOING)
        def _():
            go(k)

    for n in range(4):
        halo.arrive(UP, n)
    s[0:4] = hrecv[0, 0:4].astype(F32)

    @pl.loop(0, 4)
    def _(n):
        weigh(12 + n, s, w, HALF)
        tick(n)

    pl.loop(0, 4)(lambda n: weigh(n, s, w, HALF))

    for n in range(4):
        px_copy(n).wait_recv()

    @pl.loop(0, ROWS)
    def _(r):
        se[4 + r] = psend[r, 0:EXT, :].astype(F32) + pxrecv[r].astype(F32)

    hxsend[0:4] = se[4:8].astype(BF16)
    hxsend[4:8] = se[16:20].astype(BF16)
    halo_ext.start(DOWN)
    halo_ext.start(UP)
    grad[...] = jnp.zeros_like(grad)

    def add_grad(weights, data, total=grad):
        total[...] += lax.dot_general(
            weights, data, (((0,), (0,)), ((), ())), preferred_element_type=F32
        )

    def own_grad(n):
        some = pl.ds(pl.multiple_of(n * CH, CH), CH)
        add_grad(w[some, :], xo[some, :])

    def rest_grad(start, rows, total=grad):
        for r in range(start, start + rows):
            w_copy(r).wait_recv()
        some = slice(start * REST, (start + rows) * REST)
        add_grad(wrecv[some, :], xt[some, :], total)

    @pl.loop(0, 2)
    def _(n):
        own_grad(n)
        tick(4 + n)

    @pl.loop(2, 4)
    def _(n):
        own_grad(n)
        tick(4 + n)

    rest_grad(4, 4)
    tick(8)
    tick(9)
    tick(10)
    tick(11)
    rest_grad(8, 4)
    halo_ext.arrive(DOWN)
    halo_ext.arrive(UP)
    se[20:24] = hxrecv[0, 4:8].astype(F32)
    se[0:4] = hxrecv[0, 0:4].astype(F32)

    @pl.loop(0, ROWS)
    def _(r):
        weigh(r, se, we, EXT)

    add_grad(we[...], xe[...])
    def z_copy(j):
        return pltpu.make_async_remote_copy(
            grad.at[pl.ds(pl.multiple_of((q + j) % 8 * 8, 8), 8)], red_z.at[q],
            z_ssem, z_rsem, device_id=zc_peer(j), device_id_type=MESH,
        )

    def xx_copy(j):
        return pltpu.make_async_remote_copy(
            grad.at[pl.ds(pl.multiple_of(64 + (u + j) % 8 * 8, 8), 8)], red_x.at[u],
            xx_ssem, xx_rsem, device_id=xc_peer(j), device_id_type=MESH,
        )

    def seven(ref, send, recv):
        some = ref.at[pl.ds(0, 7)]
        return pltpu.make_async_remote_copy(
            some, some, send, recv, device_id=partner, device_id_type=MESH
        )

    @pl.loop(1, 8)
    def _(j):
        z_copy(j).start()
        xx_copy(j).start()

    late[...] = jnp.zeros_like(late)
    for start, rows in ((12, 4), (0, 2), (2, 1), (3, 1)):
        rest_grad(start, rows, late)

    for n in range(16):
        term = late[8 * n : 8 * n + 8, :]
        piece[n] = jnp.concatenate([term[:, :512], term[:, 512:]], axis=0).astype(BF16)

    def lz_copy(j):
        return pltpu.make_async_remote_copy(
            piece.at[(q + j) % 8], late_z.at[q], lz_ssem, lz_rsem,
            device_id=zc_peer(j), device_id_type=MESH,
        )

    def lx_copy(j):
        return pltpu.make_async_remote_copy(
            piece.at[8 + (u + j) % 8], late_x.at[u], lx_ssem, lx_rsem,
            device_id=xc_peer(j), device_id_type=MESH,
        )

    @pl.loop(1, 8)
    def _(j):
        lz_copy(j).start()
        lx_copy(j).start()

    late_z[q] = piece[q]
    late_x[u] = piece[8 + u]
    red_z[q] = grad[pl.ds(pl.multiple_of(q * 8, 8), 8), :]
    red_x[u] = grad[pl.ds(pl.multiple_of(64 + u * 8, 8), 8), :]

    seven(red_z, z_ssem, z_rsem).wait_recv()
    seven(red_x, xx_ssem, xx_rsem).wait_recv()
    total_z, total_x = red_z[0], red_x[0]
    for n in range(1, 8):
        total_z = total_z + red_z[n]
        total_x = total_x + red_x[n]
    seven(late_z, lz_ssem, lz_rsem).wait_recv()
    seven(late_x, lx_ssem, lx_rsem).wait_recv()

    def all_late(ref):
        term = ref[0].astype(F32)
        for n in range(1, 8):
            term = term + ref[n].astype(F32)
        return jnp.concatenate([term[0:8], term[8:16]], axis=1)

    total_z = total_z + all_late(late_z)
    total_x = total_x + all_late(late_x)
    for n in range(4):
        part[n] = total_z[2 * n : 2 * n + 2, :]
        part[4 + n] = total_x[2 * n : 2 * n + 2, :]

    def bz_copy(j):
        to = (xx + j) % 4
        return pltpu.make_async_remote_copy(
            part.at[to], red_b.at[xx * 2 + ylo], b_ssem, b_rsem,
            device_id=device_of(to, chan * 2, z, core), device_id_type=MESH,
        )

    def bx_copy(j):
        to = (z + j) % 4
        return pltpu.make_async_remote_copy(
            part.at[4 + to], red_b.at[z * 2 + ylo], b_ssem, b_rsem,
            device_id=device_of(xx, chan * 2 + 1, to, core), device_id_type=MESH,
        )

    @pl.when(ylo == 0)
    def _():
        bx_copy(0).start()
        red_b[xx * 2] = part[xx]

    @pl.when(ylo == 1)
    def _():
        bz_copy(0).start()
        red_b[z * 2 + 1] = part[4 + z]

    for j in range(1, 4):
        bz_copy(j).start()
        bx_copy(j).start()
    seven(red_b, b_ssem, b_rsem).wait_recv()
    total = red_b[0]
    for n in range(1, 8):
        total = total + red_b[n]
    g_out[...] = total

    sent_a.wait_send()
    sent_b.wait_send()

    @pl.loop(0, 4)
    def _(r):
        w_copy(r).wait_send()

    for n in range(4):
        px_copy(n).wait_send()
    for up in (False, True):
        halo.drain(up)
        halo_ext.drain(up)

    seven(red_z, z_ssem, z_rsem).wait_send()
    seven(red_x, xx_ssem, xx_rsem).wait_send()
    seven(red_b, b_ssem, b_rsem).wait_send()
    seven(late_z, lz_ssem, lz_rsem).wait_send()
    seven(late_x, lx_ssem, lx_rsem).wait_send()


def on_device(spectra, factors):
    dma = pltpu.SemaphoreType.DMA
    return pl.pallas_call(
        kernel,
        name="autocorrelation_gradient",
        out_shape=(
            jax.ShapeDtypeStruct((2, CH), F32),
            jax.ShapeDtypeStruct((1,), F32),
        ),
        in_specs=[pl.BlockSpec(memory_space=pl.ANY)] * 2,
        out_specs=(
            pl.BlockSpec(memory_space=pltpu.VMEM),
            pl.BlockSpec(memory_space=pltpu.SMEM),
        ),
        scratch_shapes=[
            pltpu.VMEM((ROWS * HALF, CH), BF16),
            pltpu.VMEM((ROWS * EXT, CH), BF16),
            pltpu.VMEM((ROWS * REST, CH), BF16),
            pltpu.VMEM((CH, K), BF16),
            pltpu.VMEM((CH, K), BF16),
            pltpu.VMEM((ROWS + 8, HALF, K), F32),
            pltpu.VMEM((ROWS + 8, EXT, K), F32),
            pltpu.VMEM((ROWS, HALF, K), BF16),
            pltpu.VMEM((ROWS, HALF, K), BF16),
            pltpu.VMEM((ROWS, EXT, K), BF16),
            pltpu.VMEM((ROWS, EXT, K), BF16),
            pltpu.VMEM((8, HALF, K), BF16),
            pltpu.VMEM((2, 8, HALF, K), BF16),
            pltpu.VMEM((8, EXT, K), BF16),
            pltpu.VMEM((2, 8, EXT, K), BF16),
            pltpu.VMEM((ROWS * HALF, K), BF16),
            pltpu.VMEM((ROWS * EXT, K), BF16),
            pltpu.VMEM((ROWS * REST, K), BF16),
            pltpu.VMEM((8, K), F32),
            pltpu.VMEM((6, 8, K), F32),
            pltpu.VMEM((8, K), F32),
            pltpu.VMEM((8, K), F32),
            pltpu.VMEM((8, 8, K), F32),
            pltpu.VMEM((16, 8, K), F32),
            pltpu.VMEM((K, CH), F32),
            pltpu.VMEM((8, 8, CH), F32),
            pltpu.VMEM((8, 8, CH), F32),
            pltpu.VMEM((8, 2, CH), F32),
            pltpu.VMEM((8, 2, CH), F32),
            pltpu.VMEM((K, CH), F32),
            pltpu.VMEM((16, 16, CH // 2), BF16),
            pltpu.VMEM((8, 16, CH // 2), BF16),
            pltpu.VMEM((8, 16, CH // 2), BF16),
            dma((3, ROWS)),
            dma,
            dma((ROWS,)), dma((ROWS,)),
            dma((4,)), dma((4,)),
            dma((2, 2, 4)), dma((2, 2, 4)),
            dma((2, 2, 1)), dma((2, 2, 1)),
            dma, dma,
            dma, dma,
            dma((ROWS,)), dma((ROWS,)),
            dma, dma,
            dma, dma,
            dma, dma,
            dma, dma,
            dma, dma,
        ],
        compiler_params=pltpu.CompilerParams(
            collective_id=0, has_side_effects=True, vmem_limit_bytes=56 << 20
        ),
    )(spectra, factors)


def solution(mesh):
    return jax.shard_map(
        on_device,
        mesh=mesh,
        in_specs=(P("rows", None, "chan"), P("chan", None)),
        out_specs=(P("rows", "chan"), P()),
        check_vma=False,
    )
```

```python
import jax
import jax.numpy as jnp
from jax import lax
from jax.experimental import pallas as pl
from jax.experimental.pallas import tpu as pltpu
from jax.sharding import PartitionSpec as P

MESH = pl.DeviceIdType.MESH
F32, BF16 = jnp.float32, jnp.bfloat16

ROWS = 16
STRIPS = 64
WP = 512
HALF = 256
EXT = 128
REST = HALF - EXT
K = 128
CH = 1024
H = ROWS * STRIPS
NPIX = float(H * WP)
LAGS = (1, 2, 3, 4)
PAIRS = tuple(float((H - lag) * WP) for lag in LAGS)
AHEAD = 4
FLYING = 8
GOING = 6
SUB = 32


def device_of(x, y, z, core):
    return ((x * 2 + y % 2) * 4 + z) * 2 + core, y // 2


def fold(block):
    return jnp.sum(block.reshape(block.shape[0] // 8, 8, K), axis=0)


def kernel(
    x_hbm, f_hbm, g_out, obj_out,
    xo, xe, xt, fv, fp, s, se, psend, precv, pxsend, pxrecv, hsend, hrecv, hxsend, hxrecv,
    w, we, wrecv, mu, acc, tile, tile_b, mom_a, mom_b, grad,
    red_z, red_x, part, red_b, late, piece, late_z, late_x,
    x_sem, f_sem, p_ssem, p_rsem, px_ssem, px_rsem, h_ssem, h_rsem, hx_ssem, hx_rsem, ma_ssem, ma_rsem, mb_ssem, mb_rsem,
    w_ssem, w_rsem, z_ssem, z_rsem, xx_ssem, xx_rsem, b_ssem, b_rsem,
    lz_ssem, lz_rsem, lx_ssem, lx_rsem,
):
    strip = lax.axis_index("rows")
    chan = lax.axis_index("chan")
    core, z, ylo, xx = strip % 2, (strip // 2) % 4, (strip // 8) % 2, strip // 16
    y = chan * 2 + ylo
    mine = pl.multiple_of(chan * HALF, HALF)
    theirs = pl.multiple_of((1 - chan) * HALF, HALF)
    partner = (strip, 1 - chan)
    after = ((strip + 1) % STRIPS, chan)
    before = ((strip + STRIPS - 1) % STRIPS, chan)

    def order(i):
        return i // 4 * 12 % ROWS + i % 4

    def x_copy(r, n):
        at, size, to = ((theirs, EXT, xe), (theirs + EXT, REST, xt), (mine, HALF, xo))[n]
        return pltpu.make_async_copy(
            x_hbm.at[r, pl.ds(pl.multiple_of(at, SUB), size), :],
            to.at[pl.ds(pl.multiple_of(r * size, SUB), size), :],
            x_sem.at[n, r],
        )

    f_copy = pltpu.make_async_copy(f_hbm, fv, f_sem)
    f_copy.start()

    for i in range(AHEAD):
        x_copy(order(i), 0).start()
        x_copy(order(i), 1).start()

    barrier = pltpu.get_barrier_semaphore()

    def greet(place):
        pl.semaphore_signal(barrier, inc=1, device_id=place, device_id_type=MESH)

    q = z * 2 + core
    t = xx * 4 + y
    u = xx * 2 + core

    def zc_peer(j):
        other = (q + j) % 8
        return device_of(xx, y, other // 2, other % 2)

    def xy_peer(j):
        other = (t + j) % 16
        return device_of(other // 4, other % 4, z, core)

    def xc_peer(j):
        other = (u + j) % 8
        return device_of(other // 2, y, z, other % 2)

    @pl.loop(1, 8)
    def _(j):
        greet(zc_peer(j))

    @pl.loop(1, 16)
    def _(j):
        greet(xy_peer(j))

    @pl.loop(1, 4)
    def _(j):
        greet(device_of((xx + j) % 4, y, z, 1 - core))
        greet(device_of(xx, chan * 2 + 1 - ylo, (z + j) % 4, core))

    @pl.when((z == 3) & (core == 1))
    def _():
        greet(after)
        greet(device_of((xx + 1) % 4, y, 0, 0))

    @pl.when((z == 0) & (core == 0))
    def _():
        greet(before)
        greet(device_of((xx + 3) % 4, y, 3, 1))

    greeted = 28 + 2 * (z // 3 * core + (3 - z) // 3 * (1 - core))

    f_copy.wait()
    src = lax.broadcasted_iota(jnp.int32, (K, K), 0)
    dst = lax.broadcasted_iota(jnp.int32, (K, K), 1)
    hi, mid, lo, e = dst >> 6, (dst >> 3) & 7, (dst >> 1) & 3, dst & 1
    to_x = jnp.where(hi == 0, lo, mid >> 1)
    to_z = jnp.where(hi == 0, mid >> 1, lo)
    from_k = (((to_x * 2 + hi) * 4 + to_z) * 2 + (mid & 1)) * 2 + e
    permutation = jnp.where(src == from_k, 1.0, 0.0).astype(BF16)
    fp[...] = jnp.dot(fv[...], permutation, preferred_element_type=F32).astype(BF16)

    def p_copy(r):
        return pltpu.make_async_remote_copy(
            psend.at[r], precv.at[r], p_ssem.at[r], p_rsem.at[r],
            device_id=partner, device_id_type=MESH,
        )

    def scores(ref, r, size):
        data = ref[pl.ds(pl.multiple_of(r * size, SUB), size), :]
        return jnp.dot(data, fp[...], preferred_element_type=F32)

    @pl.loop(0, ROWS)
    def _(i):
        r = order(i)

        @pl.when(i + AHEAD < ROWS)
        def _():
            x_copy(order(i + AHEAD), 0).start()
            x_copy(order(i + AHEAD), 1).start()

        x_copy(r, 2).start()
        x_copy(r, 0).wait()
        psend[r, 0:EXT, :] = scores(xe, r, EXT).astype(BF16)
        x_copy(r, 1).wait()
        psend[r, EXT:HALF, :] = scores(xt, r, REST).astype(BF16)

        @pl.when(i == 0)
        def _():
            pl.semaphore_wait(barrier, greeted)

        @pl.when(i < FLYING)
        def _():
            p_copy(r).start()

    acc[...] = jnp.zeros_like(acc)

    def add_row(i, first=False):
        r = order(i)
        p_copy(r).wait_send()

        @pl.when(i + FLYING < ROWS)
        def _():
            p_copy(order(i + FLYING)).start()

        x_copy(r, 2).wait()
        s[4 + r] = scores(xo, r, HALF)
        pxsend[r] = s[4 + r, 0:EXT, :].astype(BF16)
        p_copy(r).wait_recv()
        if first:
            total = jnp.zeros((8, K), F32)
            for h in range(0, HALF, SUB):
                total += fold(s[4 + r, h : h + SUB, :] + precv[r, h : h + SUB, :].astype(F32))
            mu[...] = jnp.broadcast_to(
                jnp.sum(total, axis=0, keepdims=True) * (1.0 / HALF), (8, K)
            )
        shift = mu[0:1, :]
        one, two = jnp.zeros((8, K), F32), jnp.zeros((8, K), F32)
        for h in range(0, HALF, SUB):
            v = s[4 + r, h : h + SUB, :] + precv[r, h : h + SUB, :].astype(F32)
            s[4 + r, h : h + SUB, :] = v
            d = v - shift
            one += fold(d)
            two += fold(d * d)
        acc[0] += one
        acc[1] += two

    def add_lags(a, across=None):
        sums = [jnp.zeros((8, K), F32) for _ in LAGS]
        for h in range(0, HALF, SUB):
            here = s[4 + a, h : h + SUB, :]
            for n, lag in enumerate(LAGS):
                d = s[4 + a + lag, h : h + SUB, :] - here
                sums[n] += fold(d * d)
        for n, lag in enumerate(LAGS):
            inside = across is None or a + lag < ROWS
            acc[2 + n] += sums[n] if inside else sums[n] * across

    class Halo:
        def __init__(self, size, send, hold, send_sem, recv_sem):
            self.size, self.send, self.hold, self.sems = size, send, hold, (send_sem, recv_sem)

        def copy(self, up, n, hop, source, slot, place):
            way = 0 if up else 1
            return pltpu.make_async_remote_copy(
                source, self.held(up, n, slot),
                self.sems[0].at[way, hop, n], self.sems[1].at[way, slot, n],
                device_id=place, device_id_type=MESH,
            )

        def held(self, up, n, slot):
            return self.hold.at[slot, pl.ds((0 if up else 4) + n * self.size, self.size)]

        def first(self, up, n, far=False):
            source = self.send.at[pl.ds((4 if up else 0) + n * self.size, self.size)]
            if far and (not up or self.size == 4):
                return self.copy(up, n, 0, source, 0, after if up else before)
            if far:
                return self.copy(up, n, 0, source, 1, device_of(xx, chan * 2 + 1 - ylo, z, core))
            return self.copy(up, n, 0, source, 0, zc_peer(1 if up else 7))

        def second(self, n):
            place = device_of((xx + 1 - ylo) % 4, y, 0, 0)
            return self.copy(True, n, 1, self.held(True, n, 1), 0, place)

        def end(self, up):
            return (z == 3) & (core == 1) if up else (z == 0) & (core == 0)

        def start(self, up, n=0):
            @pl.when(self.end(up))
            def _():
                self.first(up, n, far=True).start()

            @pl.when(jnp.logical_not(self.end(up)))
            def _():
                self.first(up, n).start()

        def arrive(self, up, n=0, slot=0):
            self.copy(up, n, 0, self.held(up, n, slot), slot, partner).wait_recv()

        def relay(self, n=0):
            @pl.when(self.end(True))
            def _():
                self.arrive(True, n, 1)
                self.second(n).start()

        def drain(self, up):
            @pl.loop(0, 4 // self.size)
            def _(n):
                self.first(up, n).wait_send()
                if not up or self.size == 4:
                    return

                @pl.when(self.end(up))
                def _():
                    self.second(n).wait_send()

    halo = Halo(1, hsend, hrecv, h_ssem, h_rsem)
    halo_ext = Halo(4, hxsend, hxrecv, hx_ssem, hx_rsem)
    UP, DOWN = True, False

    def px_copy(n):
        return pltpu.make_async_remote_copy(
            pxsend.at[pl.ds(n * 4, 4)], pxrecv.at[pl.ds(n * 4, 4)], px_ssem.at[n], px_rsem.at[n],
            device_id=partner, device_id_type=MESH,
        )

    def send_down(n):
        hsend[n] = s[4 + n].astype(BF16)
        halo.start(DOWN, n)

    add_row(0, first=True)
    send_down(0)

    @pl.loop(1, 4)
    def _(n):
        add_row(n)
        send_down(n)

    @pl.loop(0, 4)
    def _(n):
        add_row(4 + n)
        hsend[4 + n] = s[16 + n].astype(BF16)
        halo.start(UP, n)

    @pl.loop(0, 4)
    def _(n):
        add_row(8 + n)

    @pl.loop(8, 12)
    def _(a):
        add_lags(a)

    @pl.loop(0, 3)
    def _(n):
        add_row(12 + n)
        add_lags(n)

    px_copy(0).start()
    for n in range(4):
        halo.arrive(DOWN, n)
    s[20:24] = hrecv[0, 4:8].astype(F32)
    inner = jnp.where(strip == STRIPS - 1, 0.0, 1.0).astype(F32)
    for a in range(12, 16):
        add_lags(a, inner)
    add_row(15)
    px_copy(3).start()

    @pl.loop(3, 8)
    def _(a):
        add_lags(a)

    count = float(ROWS * HALF)
    drift = jnp.sum(acc[0], axis=0, keepdims=True) * (1.0 / count)
    tile[0:1] = mu[0:1, :] + drift
    tile[1:2] = jnp.sum(acc[1], axis=0, keepdims=True) - count * drift * drift
    for n in range(4):
        tile[2 + n : 3 + n] = jnp.sum(acc[2 + n], axis=0, keepdims=True)
    tile[6:8] = jnp.zeros((2, K), F32)

    def gather(tile, size, me, peer, slots, send, recv, beside):
        slots[me] = tile[...]

        def copies(source, target, place):
            return pltpu.make_async_remote_copy(
                source, target, send, recv, device_id=place, device_id_type=MESH
            )

        @pl.loop(1, size)
        def _(j):
            copies(tile, slots.at[me], peer(j)).start()

        px_copy(beside).start()
        others = slots.at[pl.ds(0, size - 1)]
        copies(others, others, partner).wait_recv()
        return copies(others, others, partner)

    def merge(slots, size, each):
        parts = [slots[n] for n in range(size)]
        total = parts[0]
        for part_ in parts[1:]:
            total = total + part_
        mean = total[0:1] * (1.0 / size)
        spread = jnp.zeros((1, K), F32)
        for part_ in parts:
            gap = part_[0:1] - mean
            spread += gap * gap
        return mean, total[1:2] + each * spread, total[2:6]

    sent_a = gather(tile, 8, q, zc_peer, mom_a, ma_ssem, ma_rsem, 2)
    mean, squares, lags = merge(mom_a, 8, count)
    tile_b[0:1] = mean
    tile_b[1:2] = squares
    tile_b[2:6] = lags
    tile_b[6:8] = jnp.zeros((2, K), F32)
    sent_b = gather(tile_b, 16, t, xy_peer, mom_b, mb_ssem, mb_rsem, 1)
    mean, squares, lags = merge(mom_b, 16, 8 * count)
    cov = jnp.sum(squares, axis=1, keepdims=True) * (1.0 / NPIX)
    variogram = jnp.zeros((1, 1), F32)
    for n in range(4):
        variogram += jnp.sum(lags[n : n + 1], axis=1, keepdims=True) / (2.0 * PAIRS[n])
    objective = variogram / cov
    obj_out[0] = objective[0, 0]
    alpha = [jnp.broadcast_to((NPIX / n) / cov, (1, K)) for n in PAIRS]
    beta = jnp.broadcast_to(2.0 * objective / cov, (1, K))

    for n in range(4):
        halo.relay(n)

    def w_copy(r):
        return pltpu.make_async_remote_copy(
            w.at[pl.ds(pl.multiple_of(r * HALF + EXT, SUB), REST)],
            wrecv.at[pl.ds(pl.multiple_of(r * REST, SUB), REST)], w_ssem.at[r], w_rsem.at[r],
            device_id=partner, device_id_type=MESH,
        )

    def weigh(r, source, target, size):
        row = strip * ROWS + r
        back = [alpha[n] * jnp.where(row >= lag, 1.0, 0.0) for n, lag in enumerate(LAGS)]
        ahead = [alpha[n] * jnp.where(row + lag < H, 1.0, 0.0) for n, lag in enumerate(LAGS)]
        for h in range(0, size, SUB):
            here = source[4 + r, h : h + SUB, :]
            value = beta * (mean - here)
            for n, lag in enumerate(LAGS):
                value += back[n] * (here - source[4 + r - lag, h : h + SUB, :])
                value += ahead[n] * (here - source[4 + r + lag, h : h + SUB, :])
            target[pl.ds(pl.multiple_of(r * size + h, SUB), SUB), :] = value.astype(BF16)

    def go(k):
        w_copy((k + 4) % ROWS).start()

    def tick(k):
        w_copy((k + 4) % ROWS).wait_send()
        if isinstance(k, int):
            if k + GOING < ROWS:
                go(k + GOING)
        else:
            pl.when(k + GOING < ROWS)(lambda: go(k + GOING))

    @pl.loop(0, 8)
    def _(k):
        weigh(k + 4, s, w, HALF)

        @pl.when(k < GOING)
        def _():
            go(k)

    for n in range(4):
        halo.arrive(UP, n)
    s[0:4] = hrecv[0, 0:4].astype(F32)

    @pl.loop(0, 4)
    def _(n):
        weigh(12 + n, s, w, HALF)
        tick(n)

    pl.loop(0, 4)(lambda n: weigh(n, s, w, HALF))

    for n in range(4):
        px_copy(n).wait_recv()

    @pl.loop(0, ROWS)
    def _(r):
        se[4 + r] = psend[r, 0:EXT, :].astype(F32) + pxrecv[r].astype(F32)

    hxsend[0:4] = se[4:8].astype(BF16)
    hxsend[4:8] = se[16:20].astype(BF16)
    halo_ext.start(DOWN)
    halo_ext.start(UP)
    grad[...] = jnp.zeros_like(grad)

    def add_grad(weights, data, total=grad):
        total[...] += lax.dot_general(
            weights, data, (((0,), (0,)), ((), ())), preferred_element_type=F32
        )

    def own_grad(n):
        some = pl.ds(pl.multiple_of(n * CH, CH), CH)
        add_grad(w[some, :], xo[some, :])

    def rest_grad(start, rows, total=grad):
        for r in range(start, start + rows):
            w_copy(r).wait_recv()
        some = slice(start * REST, (start + rows) * REST)
        add_grad(wrecv[some, :], xt[some, :], total)

    @pl.loop(0, 2)
    def _(n):
        own_grad(n)
        tick(4 + n)

    @pl.loop(2, 4)
    def _(n):
        own_grad(n)
        tick(4 + n)

    rest_grad(4, 4)
    tick(8)
    tick(9)
    tick(10)
    tick(11)
    rest_grad(8, 4)
    halo_ext.arrive(DOWN)
    halo_ext.arrive(UP)
    se[20:24] = hxrecv[0, 4:8].astype(F32)
    se[0:4] = hxrecv[0, 0:4].astype(F32)

    @pl.loop(0, ROWS)
    def _(r):
        weigh(r, se, we, EXT)

    add_grad(we[...], xe[...])
    def z_copy(j):
        return pltpu.make_async_remote_copy(
            grad.at[pl.ds(pl.multiple_of((q + j) % 8 * 8, 8), 8)], red_z.at[q],
            z_ssem, z_rsem, device_id=zc_peer(j), device_id_type=MESH,
        )

    def xx_copy(j):
        return pltpu.make_async_remote_copy(
            grad.at[pl.ds(pl.multiple_of(64 + (u + j) % 8 * 8, 8), 8)], red_x.at[u],
            xx_ssem, xx_rsem, device_id=xc_peer(j), device_id_type=MESH,
        )

    def seven(ref, send, recv):
        some = ref.at[pl.ds(0, 7)]
        return pltpu.make_async_remote_copy(
            some, some, send, recv, device_id=partner, device_id_type=MESH
        )

    @pl.loop(1, 8)
    def _(j):
        z_copy(j).start()
        xx_copy(j).start()

    late[...] = jnp.zeros_like(late)
    for start, rows in ((12, 4), (0, 2), (2, 1), (3, 1)):
        rest_grad(start, rows, late)

    for n in range(16):
        term = late[8 * n : 8 * n + 8, :]
        piece[n] = jnp.concatenate([term[:, :512], term[:, 512:]], axis=0).astype(BF16)

    def lz_copy(j):
        return pltpu.make_async_remote_copy(
            piece.at[(q + j) % 8], late_z.at[q], lz_ssem, lz_rsem,
            device_id=zc_peer(j), device_id_type=MESH,
        )

    def lx_copy(j):
        return pltpu.make_async_remote_copy(
            piece.at[8 + (u + j) % 8], late_x.at[u], lx_ssem, lx_rsem,
            device_id=xc_peer(j), device_id_type=MESH,
        )

    @pl.loop(1, 8)
    def _(j):
        lz_copy(j).start()
        lx_copy(j).start()

    late_z[q] = piece[q]
    late_x[u] = piece[8 + u]
    red_z[q] = grad[pl.ds(pl.multiple_of(q * 8, 8), 8), :]
    red_x[u] = grad[pl.ds(pl.multiple_of(64 + u * 8, 8), 8), :]

    seven(red_z, z_ssem, z_rsem).wait_recv()
    seven(red_x, xx_ssem, xx_rsem).wait_recv()
    total_z, total_x = red_z[0], red_x[0]
    for n in range(1, 8):
        total_z = total_z + red_z[n]
        total_x = total_x + red_x[n]
    seven(late_z, lz_ssem, lz_rsem).wait_recv()
    seven(late_x, lx_ssem, lx_rsem).wait_recv()

    def all_late(ref):
        term = ref[0].astype(F32)
        for n in range(1, 8):
            term = term + ref[n].astype(F32)
        return jnp.concatenate([term[0:8], term[8:16]], axis=1)

    total_z = total_z + all_late(late_z)
    total_x = total_x + all_late(late_x)
    for n in range(4):
        part[n] = total_z[2 * n : 2 * n + 2, :]
        part[4 + n] = total_x[2 * n : 2 * n + 2, :]

    def bz_copy(j):
        to = (xx + j) % 4
        return pltpu.make_async_remote_copy(
            part.at[to], red_b.at[xx * 2 + ylo], b_ssem, b_rsem,
            device_id=device_of(to, chan * 2, z, core), device_id_type=MESH,
        )

    def bx_copy(j):
        to = (z + j) % 4
        return pltpu.make_async_remote_copy(
            part.at[4 + to], red_b.at[z * 2 + ylo], b_ssem, b_rsem,
            device_id=device_of(xx, chan * 2 + 1, to, core), device_id_type=MESH,
        )

    @pl.when(ylo == 0)
    def _():
        bx_copy(0).start()
        red_b[xx * 2] = part[xx]

    @pl.when(ylo == 1)
    def _():
        bz_copy(0).start()
        red_b[z * 2 + 1] = part[4 + z]

    for j in range(1, 4):
        bz_copy(j).start()
        bx_copy(j).start()
    seven(red_b, b_ssem, b_rsem).wait_recv()
    total = red_b[0]
    for n in range(1, 8):
        total = total + red_b[n]
    g_out[...] = total

    sent_a.wait_send()
    sent_b.wait_send()

    @pl.loop(0, 4)
    def _(r):
        w_copy(r).wait_send()

    for n in range(4):
        px_copy(n).wait_send()
    for up in (False, True):
        halo.drain(up)
        halo_ext.drain(up)

    seven(red_z, z_ssem, z_rsem).wait_send()
    seven(red_x, xx_ssem, xx_rsem).wait_send()
    seven(red_b, b_ssem, b_rsem).wait_send()
    seven(late_z, lz_ssem, lz_rsem).wait_send()
    seven(late_x, lx_ssem, lx_rsem).wait_send()


def on_device(spectra, factors):
    dma = pltpu.SemaphoreType.DMA
    return pl.pallas_call(
        kernel,
        name="autocorrelation_gradient",
        out_shape=(
            jax.ShapeDtypeStruct((2, CH), F32),
            jax.ShapeDtypeStruct((1,), F32),
        ),
        in_specs=[pl.BlockSpec(memory_space=pl.ANY)] * 2,
        out_specs=(
            pl.BlockSpec(memory_space=pltpu.VMEM),
            pl.BlockSpec(memory_space=pltpu.SMEM),
        ),
        scratch_shapes=[
            pltpu.VMEM((ROWS * HALF, CH), BF16),
            pltpu.VMEM((ROWS * EXT, CH), BF16),
            pltpu.VMEM((ROWS * REST, CH), BF16),
            pltpu.VMEM((CH, K), BF16),
            pltpu.VMEM((CH, K), BF16),
            pltpu.VMEM((ROWS + 8, HALF, K), F32),
            pltpu.VMEM((ROWS + 8, EXT, K), F32),
            pltpu.VMEM((ROWS, HALF, K), BF16),
            pltpu.VMEM((ROWS, HALF, K), BF16),
            pltpu.VMEM((ROWS, EXT, K), BF16),
            pltpu.VMEM((ROWS, EXT, K), BF16),
            pltpu.VMEM((8, HALF, K), BF16),
            pltpu.VMEM((2, 8, HALF, K), BF16),
            pltpu.VMEM((8, EXT, K), BF16),
            pltpu.VMEM((2, 8, EXT, K), BF16),
            pltpu.VMEM((ROWS * HALF, K), BF16),
            pltpu.VMEM((ROWS * EXT, K), BF16),
            pltpu.VMEM((ROWS * REST, K), BF16),
            pltpu.VMEM((8, K), F32),
            pltpu.VMEM((6, 8, K), F32),
            pltpu.VMEM((8, K), F32),
            pltpu.VMEM((8, K), F32),
            pltpu.VMEM((8, 8, K), F32),
            pltpu.VMEM((16, 8, K), F32),
            pltpu.VMEM((K, CH), F32),
            pltpu.VMEM((8, 8, CH), F32),
            pltpu.VMEM((8, 8, CH), F32),
            pltpu.VMEM((8, 2, CH), F32),
            pltpu.VMEM((8, 2, CH), F32),
            pltpu.VMEM((K, CH), F32),
            pltpu.VMEM((16, 16, CH // 2), BF16),
            pltpu.VMEM((8, 16, CH // 2), BF16),
            pltpu.VMEM((8, 16, CH // 2), BF16),
            dma((3, ROWS)),
            dma,
            dma((ROWS,)), dma((ROWS,)),
            dma((4,)), dma((4,)),
            dma((2, 2, 4)), dma((2, 2, 4)),
            dma((2, 2, 1)), dma((2, 2, 1)),
            dma, dma,
            dma, dma,
            dma((ROWS,)), dma((ROWS,)),
            dma, dma,
            dma, dma,
            dma, dma,
            dma, dma,
            dma, dma,
        ],
        compiler_params=pltpu.CompilerParams(
            collective_id=0, has_side_effects=True, vmem_limit_bytes=56 << 20
        ),
    )(spectra, factors)


def solution(mesh):
    return jax.shard_map(
        on_device,
        mesh=mesh,
        in_specs=(P("rows", None, "chan"), P("chan", None)),
        out_specs=(P("rows", "chan"), P()),
        check_vma=False,
    )
```
